32 devices in a mesh: gz: 16 (over z, x, core), ord: 2 (over y).
Axes of the slice: x: 2, y: 2, z: 4, core: 2. Of those that a mesh axis runs over, the one named last changes fastest.
Arguments:
- initial: float32 [96, 32, 128, 128], P('ord', 'gz'), may hold values from -1 to 1
- cotangent: float32 [96, 32, 128, 128], P('ord', 'gz'), may hold values from -6 to 6
- mobility: float32 [96], P('ord'), may hold values from 0.05 to 0.15
- stiffness: float32 [96], P('ord'), may hold values from 0.5 to 1
Outputs:
- adjoint_initial: float32 [96, 32, 128, 128], P('ord', 'gz')
The draws below stay inside these ranges and needn't reach their ends.
All inputs are finite; a program needn't handle non-finite values.
Results may differ from the reference program's by a relative error of at most 0.00002.
Values sent between devices are 32-bit elements; how exact they have to be, the bound alone decides.
No kernel may reach another device: no remote copies, remote signals or barrier semaphores. Data moves between devices by JAX's collectives and lax.ppermute only.
A program may use at most 192 MiB of HBM per device.

```python
import math
import jax
import jax.numpy as jnp

P_SIZE = 96
NX = 128
NY = 128
NZ = 32


def block_levels(stream_key, shape, pieces, low, largest):
    def one(position, parts):
        draws = jax.random.uniform(jax.random.fold_in(jax.random.fold_in(stream_key, 6), position), (parts,), jnp.float32, low / len(pieces), largest / len(pieces))
        return jnp.repeat(jnp.exp(draws), shape[position] // parts).reshape((-1,) + (1,) * (len(shape) - position - 1))

    factor_of = one(*pieces[0])
    for cut in pieces[1:]:
        factor_of = factor_of * one(*cut)
    return factor_of


def centred(own_key, shape, deviation, limit, split=(), kind=jnp.bfloat16):
    result = deviation * jax.random.normal(own_key, shape, jnp.float32)
    if split:
        result = result * block_levels(own_key, shape, split, -0.22, 0.18)
    return jnp.clip(result, -limit, limit).astype(kind)


def setup_inputs(seed: int = 0) -> dict:
    splits = jax.random.split(jax.random.key(seed), 5)
    initial = jnp.clip(jax.random.uniform(splits[0], (P_SIZE, NZ, NX, NY), jnp.float32, -1.0, 1.0) * block_levels(splits[0], (P_SIZE, NZ, NX, NY), ((0, 2), (1, 16)), -0.4, 0.0), -1.0, 1.0)
    cotangent = centred(splits[1], (P_SIZE, NZ, NX, NY), 1.0, 6.0, ((0, 2), (1, 16)), jnp.float32)
    mobility = jnp.clip(jnp.exp(math.log(0.15) - 1.0986123 * jax.random.uniform(splits[2], (P_SIZE,), jnp.float32) ** block_levels(splits[2], (P_SIZE,), ((0, 2),), -0.2, 0.2)), 0.05, 0.15)
    stiffness = jnp.clip(jnp.exp(math.log(1.0) - 0.6931472 * jax.random.uniform(splits[3], (P_SIZE,), jnp.float32) ** block_levels(splits[3], (P_SIZE,), ((0, 2),), -0.2, 0.2)), 0.5, 1.0)
    return dict(initial=initial, cotangent=cotangent, mobility=mobility, stiffness=stiffness)


couple_scale = 2.0


def laplacian(values):
    summed = -6.0 * values
    for axis_num in (1, 2, 3):
        summed = summed + jnp.roll(values, 1, axis_num) + jnp.roll(values, -1, axis_num)
    return summed


def forward(values, squares, rate_col, stiff_col, coupling):
    potential = -values + values * values * values + 2.0 * coupling * values * (squares - values * values) - stiff_col * laplacian(values)
    return values - rate_col * potential


def backward(values, adjoint, squares, rate_col, stiff_col, coupling):
    scaled = rate_col * adjoint
    coupled = jnp.sum(values * scaled, 0)
    well_slope = -1.0 + 3.0 * values * values + 2.0 * coupling * squares - 6.0 * coupling * values * values
    return adjoint - (well_slope * scaled + 4.0 * coupling * values * coupled - stiff_col * laplacian(scaled))


def reference(initial, cotangent, mobility, stiffness):
    coupling = couple_scale / P_SIZE
    rate_col = mobility.reshape(-1, 1, 1, 1)
    stiff_col = stiffness.reshape(-1, 1, 1, 1)
    squares_first = jnp.sum(initial * initial, 0)
    middle = forward(initial, squares_first, rate_col, stiff_col, coupling)
    squares_second = jnp.sum(middle * middle, 0)
    adjoint_middle = backward(middle, cotangent, squares_second, rate_col, stiff_col, coupling)
    return backward(initial, adjoint_middle, squares_first, rate_col, stiff_col, coupling)
```

```python
import functools

import jax
import jax.numpy as jnp
from jax import lax
from jax.experimental import pallas as pl
from jax.experimental.pallas import tpu as pltpu
from jax.sharding import PartitionSpec as P

couple_scale = 2.0
PIECES = 8
IN_FLIGHT = 4


def pieces_of(orders):
    count = min(PIECES, orders)
    while orders % count:
        count -= 1
    return count, orders // count


def inner_pairs(count):
    return [(i, i ^ 1) for i in range(count)]


def outer_pairs(count):
    return [(i, (i + 1) % count if i % 2 else (i - 1) % count) for i in range(count)]


def order_sum(values):
    count = lax.axis_size("ord")
    if count & (count - 1):
        return lax.psum(values, "ord")
    step = 1
    while step < count:
        values = values + lax.ppermute(values, "ord", [(i, i ^ step) for i in range(count)])
        step *= 2
    return values


def in_plane(plane):
    rows, columns = plane.shape
    return (
        pltpu.roll(plane, 1, 0)
        + pltpu.roll(plane, rows - 1, 0)
        + pltpu.roll(plane, 1, 1)
        + pltpu.roll(plane, columns - 1, 1)
    )


def place(odd, position, planes):
    return position + odd * (planes - 1 - 2 * position)


def middle_kernel(base, planes, coupling, fresh, odd_ref, rate_ref, stiff_ref, field, adjoint, far, near, squares, *rest):
    if fresh:
        middle, sums = rest
    else:
        sums_before, middle, sums = rest
    step = pl.program_id(0)
    rate = rate_ref[base + step]
    stiff = rate * stiff_ref[base + step]
    odd = odd_ref[0]

    @pl.when(step == 0)
    def _():
        sums[...] = jnp.zeros_like(sums) if fresh else sums_before[...]

    for position in range(planes):
        z = place(odd, position, planes)
        centre = field[0, z]
        before = far[0] if position == 0 else field[0, place(odd, position - 1, planes)]
        after = near[0] if position == planes - 1 else field[0, place(odd, position + 1, planes)]
        around = in_plane(centre) + (before + after)
        factor = (1.0 + rate - 6.0 * stiff) - rate * (
            (2.0 * coupling) * squares[z] + (1.0 - 2.0 * coupling) * (centre * centre)
        )
        value = centre * factor + stiff * around
        middle[0, z] = value
        sums[0, z] += value * value
        sums[1, z] += value * (rate * adjoint[0, z])


def pulled_back(rate, stiff, coupling, value, adjoint, around, squares, coupled):
    factor = (1.0 + rate - 6.0 * stiff) - rate * (
        (2.0 * coupling) * squares + (3.0 - 6.0 * coupling) * (value * value)
    )
    return adjoint * factor - (4.0 * coupling) * (value * coupled) + stiff * around


def adjoint_kernel(base, planes, coupling, fresh, odd_ref, rate_ref, stiff_ref, field, middle, adjoint, far, near, sums, *rest):
    if fresh:
        outs, coupled = rest[:planes], rest[planes]
    else:
        coupled_before, outs, coupled = rest[0], rest[1:planes + 1], rest[planes + 1]
    step = pl.program_id(0)
    rate = rate_ref[base + step]
    stiff = rate * stiff_ref[base + step]
    odd = odd_ref[0]

    @pl.when(step == 0)
    def _():
        coupled[...] = jnp.zeros_like(coupled) if fresh else coupled_before[...]

    for position in range(planes):
        z = place(odd, position, planes)
        centre = adjoint[0, z]
        before = far[0] if position == 0 else adjoint[0, place(odd, position - 1, planes)]
        after = near[0] if position == planes - 1 else adjoint[0, place(odd, position + 1, planes)]
        around = in_plane(centre) + (before + after)
        value = pulled_back(rate, stiff, coupling, middle[0, z], centre, around, sums[0, z], sums[1, z])
        outs[position][0] = value
        coupled[z] += field[0, z] * (rate * value)


def last_kernel(base, planes, coupling, fresh, odd_ref, rate_ref, stiff_ref, field, far, near, squares, coupled, *rest):
    adjoint = rest[:planes]
    out = rest[-1]
    step = pl.program_id(0)
    rate = rate_ref[base + step]
    stiff = rate * stiff_ref[base + step]
    odd = odd_ref[0]
    for position in range(planes):
        z = place(odd, position, planes)
        centre = adjoint[position][0]
        before = far[0] if position == 0 else adjoint[position - 1][0]
        after = near[0] if position == planes - 1 else adjoint[position + 1][0]
        around = in_plane(centre) + (before + after)
        out[0, z] = pulled_back(rate, stiff, coupling, field[0, z], centre, around, squares[z], coupled[z])


def on_device(initial, cotangent, mobility, stiffness):
    orders, planes, rows, columns = initial.shape
    coupling = couple_scale / (orders * lax.axis_size("ord"))
    count, size = pieces_of(orders)
    ring = lax.axis_size("gz")
    odd = lax.rem(lax.axis_index("gz"), 2)
    odd_arr = odd.reshape(1).astype(jnp.int32)
    far_plane = odd * (planes - 1)
    near_plane = (planes - 1) - far_plane

    def send_far(plane):
        return lax.ppermute(plane, "gz", outer_pairs(ring))

    def send_near(plane):
        return lax.ppermute(plane, "gz", inner_pairs(ring))

    def cut(array, plane, start, length):
        return lax.dynamic_slice(array, (start, plane, 0, 0), (length, 1, rows, columns)).reshape(length, rows, columns)

    sent = []

    def queue(plane):
        if len(sent) >= IN_FLIGHT:
            plane, _ = lax.optimization_barrier((plane, sent[-IN_FLIGHT]))
        sent.append(send_far(plane))
        return sent[-1]

    scalar = pl.BlockSpec(memory_space=pltpu.SMEM)
    one_slab = (1, planes, rows, columns)
    one_plane = (1, rows, columns)
    slab = jax.ShapeDtypeStruct((size, planes, rows, columns), jnp.float32)
    plane_out = jax.ShapeDtypeStruct((size, rows, columns), jnp.float32)
    whole = jax.ShapeDtypeStruct(initial.shape, jnp.float32)
    cell = jax.ShapeDtypeStruct((planes, rows, columns), jnp.float32)
    cells = jax.ShapeDtypeStruct((2, planes, rows, columns), jnp.float32)
    own_slab = pl.BlockSpec(one_slab, lambda i: (i, 0, 0, 0))
    own_plane = pl.BlockSpec(one_plane, lambda i: (i, 0, 0))
    cell_spec = pl.BlockSpec(cell.shape, lambda i: (0, 0, 0))
    cells_spec = pl.BlockSpec(cells.shape, lambda i: (0, 0, 0, 0))

    def slab_at(base):
        return pl.BlockSpec(one_slab, lambda i: (base + i, 0, 0, 0))

    def plane_at(base):
        return pl.BlockSpec(one_plane, lambda i: (base + i, 0, 0))

    def call(kernel, piece, fresh, in_specs, args, out_specs, out_shape, alias, work):
        elements = size * planes * rows * columns
        return pl.pallas_call(
            functools.partial(kernel, piece * size, planes, coupling, fresh),
            grid=(size,),
            in_specs=[scalar] * 3 + in_specs,
            out_specs=out_specs,
            out_shape=out_shape,
            input_output_aliases=alias,
            cost_estimate=pl.CostEstimate(flops=work * elements, bytes_accessed=20 * elements, transcendentals=0),
            compiler_params=pltpu.CompilerParams(
                dimension_semantics=("arbitrary",), vmem_limit_bytes=32 * 1024 * 1024
            ),
        )(odd_arr, mobility, stiffness, *args)

    field_far = [queue(cut(initial, far_plane, k * size, size)) for k in range(count)]
    field_near = send_near(cut(initial, near_plane, 0, orders))
    squares_first = order_sum(jnp.sum(initial * initial, 0))
    adjoint_far = [queue(cut(cotangent, far_plane, k * size, size)) for k in range(count)]
    adjoint_near = send_near(cut(cotangent, near_plane, 0, orders))

    middle, sums = [], None
    for k in range(count):
        fresh = k == 0
        value, sums = call(
            middle_kernel, k, fresh,
            [slab_at(k * size), slab_at(k * size), own_plane, plane_at(k * size), cell_spec] + ([] if fresh else [cells_spec]),
            [initial, cotangent, field_far[k], field_near, squares_first] + ([] if fresh else [sums]),
            [own_slab, cells_spec], [slab, cells], {} if fresh else {8: 1}, 30,
        )
        middle.append(value)
    sums = order_sum(sums)

    outs, coupled = [], None
    far, near = [], []
    for k in range(count):
        fresh = k == 0
        *values, coupled = call(
            adjoint_kernel, k, fresh,
            [slab_at(k * size), own_slab, slab_at(k * size), own_plane, plane_at(k * size), cells_spec]
            + ([] if fresh else [cell_spec]),
            [initial, middle[k], cotangent, adjoint_far[k], adjoint_near, sums] + ([] if fresh else [coupled]),
            [own_plane] * planes + [cell_spec], [plane_out] * planes + [cell], {} if fresh else {9: planes}, 30,
        )
        outs.append(values)
        far.append(queue(values[0]))
        near.append(send_near(values[-1]))
    coupled = order_sum(coupled)

    result = None
    for k in range(count):
        fresh = k == 0
        result = call(
            last_kernel, k, fresh,
            [slab_at(k * size), own_plane, own_plane, cell_spec, cell_spec] + [own_plane] * planes
            + ([] if fresh else [pl.BlockSpec(memory_space=pl.ANY)]),
            [initial, far[k], near[k], squares_first, coupled] + outs[k] + ([] if fresh else [result]),
            slab_at(k * size), whole, {} if fresh else {8 + planes: 0}, 30,
        )
    return result


def solution(mesh):
    return jax.shard_map(
        on_device,
        mesh=mesh,
        in_specs=(P("ord", "gz", None, None), P("ord", "gz", None, None), P("ord"), P("ord")),
        out_specs=P("ord", "gz", None, None),
        check_vma=False,
    )
```

```python
import functools
import math

import jax
import jax.numpy as jnp
from jax import lax
from jax.experimental import pallas as pl
from jax.experimental.pallas import tpu as pltpu
from jax.sharding import PartitionSpec as P

couple_scale = 2.0
PIECES = 8
IN_FLIGHT = 3
STEP_ORDERS = 3
WORK = 30
BYTES = 120
BACK = 6
NEAR_SHARE = 1
NEAR_LAG = 2
FIRST = True
BACK_SHARE = 8
BACK_LAG = 0
AHEAD = 4


def pieces_of(orders):
    count = min(PIECES, orders)
    while orders % count:
        count -= 1
    return count, orders // count


def inner_pairs(count):
    return [(i, i ^ 1) for i in range(count)]


def outer_pairs(count):
    return [(i, (i + 1) % count if i % 2 else (i - 1) % count) for i in range(count)]


def order_sum(values):
    count = lax.axis_size("ord")
    if count & (count - 1):
        return lax.psum(values, "ord")
    step = 1
    while step < count:
        values = values + lax.ppermute(values, "ord", [(i, i ^ step) for i in range(count)])
        step *= 2
    return values


def in_plane(plane):
    rows, columns = plane.shape
    return (
        pltpu.roll(plane, 1, 0)
        + pltpu.roll(plane, rows - 1, 0)
        + pltpu.roll(plane, 1, 1)
        + pltpu.roll(plane, columns - 1, 1)
    )


def place(odd, position, planes):
    return position + odd * (planes - 1 - 2 * position)


def middle_kernel(base, planes, coupling, fresh, odd_ref, rate_ref, stiff_ref, field, adjoint, far, near, squares, *rest):
    if fresh:
        middle, sums = rest
    else:
        sums_before, middle, sums = rest
    step = pl.program_id(0)
    block = field.shape[0]
    odd = odd_ref[0]

    @pl.when(step == 0)
    def _():
        sums[...] = jnp.zeros_like(sums) if fresh else sums_before[...]

    for position in range(planes):
        z = place(odd, position, planes)
        squared, coupled = sums[0, z], sums[1, z]
        scaled_squares = (2.0 * coupling) * squares[z]
        for p in range(block):
            rate = rate_ref[base + step * block + p]
            stiff = rate * stiff_ref[base + step * block + p]
            centre = field[p, z]
            before = far[p] if position == 0 else field[p, place(odd, position - 1, planes)]
            after = near[p] if position == planes - 1 else field[p, place(odd, position + 1, planes)]
            around = in_plane(centre) + (before + after)
            factor = (1.0 + rate - 6.0 * stiff) - rate * (
                scaled_squares + (1.0 - 2.0 * coupling) * (centre * centre)
            )
            value = centre * factor + stiff * around
            middle[p, z] = value
            squared = squared + value * value
            coupled = coupled + value * (rate * adjoint[p, z])
        sums[0, z] = squared
        sums[1, z] = coupled


def pulled_back(rate, stiff, coupling, value, adjoint, around, squares, coupled):
    factor = (1.0 + rate - 6.0 * stiff) - rate * (squares + (3.0 - 6.0 * coupling) * (value * value))
    return adjoint * factor - value * coupled + stiff * around


def adjoint_kernel(base, planes, coupling, fresh, odd_ref, rate_ref, stiff_ref, field, middle, adjoint, far, near, sums, *rest):
    if fresh:
        outs, coupled = rest[-planes - 1:-1], rest[-1]
    else:
        coupled_before, outs, coupled = rest[0], rest[-planes - 1:-1], rest[-1]
    step = pl.program_id(0)
    block = field.shape[0]
    odd = odd_ref[0]

    @pl.when(step == 0)
    def _():
        coupled[...] = jnp.zeros_like(coupled) if fresh else coupled_before[...]

    for position in range(planes):
        z = place(odd, position, planes)
        total = coupled[z]
        squares, pull = (2.0 * coupling) * sums[0, z], (4.0 * coupling) * sums[1, z]
        for p in range(block):
            rate = rate_ref[base + step * block + p]
            stiff = rate * stiff_ref[base + step * block + p]
            centre = adjoint[p, z]
            before = far[p] if position == 0 else adjoint[p, place(odd, position - 1, planes)]
            after = near[p] if position == planes - 1 else adjoint[p, place(odd, position + 1, planes)]
            around = in_plane(centre) + (before + after)
            value = pulled_back(rate, stiff, coupling, middle[p, z], centre, around, squares, pull)
            outs[position][p] = value
            total = total + field[p, z] * (rate * value)
        coupled[z] = total


def last_kernel(base, planes, coupling, fresh, odd_ref, rate_ref, stiff_ref, field, far, near, squares, coupled, *rest):
    adjoint = rest[:planes]
    out, token = rest[-2:]
    token[...] = jnp.zeros_like(token)
    step = pl.program_id(0)
    block = field.shape[0]
    odd = odd_ref[0]
    for position in range(planes):
        z = place(odd, position, planes)
        scaled, pull = (2.0 * coupling) * squares[z], (4.0 * coupling) * coupled[z]
        for p in range(block):
            rate = rate_ref[base + step * block + p]
            stiff = rate * stiff_ref[base + step * block + p]
            centre = adjoint[position][p]
            before = far[p] if position == 0 else adjoint[position - 1][p]
            after = near[p] if position == planes - 1 else adjoint[position + 1][p]
            around = in_plane(centre) + (before + after)
            out[p, z] = pulled_back(rate, stiff, coupling, field[p, z], centre, around, scaled, pull)


def on_device(initial, cotangent, mobility, stiffness):
    orders, planes, rows, columns = initial.shape
    coupling = couple_scale / (orders * lax.axis_size("ord"))
    count, size = pieces_of(orders)
    block = math.gcd(size, STEP_ORDERS)
    ring = lax.axis_size("gz")
    odd = lax.rem(lax.axis_index("gz"), 2)
    odd_arr = odd.reshape(1).astype(jnp.int32)
    far_plane = odd * (planes - 1)
    near_plane = (planes - 1) - far_plane

    def send_far(plane):
        return lax.ppermute(plane, "gz", outer_pairs(ring))

    def send_near(plane):
        return lax.ppermute(plane, "gz", inner_pairs(ring))

    def cut(array, plane, start, length):
        return lax.dynamic_slice(array, (start, plane, 0, 0), (length, 1, rows, columns)).reshape(length, rows, columns)

    def after(value, *before):
        return lax.optimization_barrier((value, before))[0] if before else value

    scalar = pl.BlockSpec(memory_space=pltpu.SMEM)
    anywhere = pl.BlockSpec(memory_space=pl.ANY)
    one_slab = (block, planes, rows, columns)
    one_plane = (block, rows, columns)

    def shape(*dims):
        return jax.ShapeDtypeStruct(dims, jnp.float32)

    slab = shape(size, planes, rows, columns)
    plane_out = shape(size, rows, columns)
    cell = shape(planes, rows, columns)
    cells = shape(2, planes, rows, columns)
    cell_spec = pl.BlockSpec(cell.shape, lambda i: (0, 0, 0))
    cells_spec = pl.BlockSpec(cells.shape, lambda i: (0, 0, 0, 0))

    def slab_at(base):
        return pl.BlockSpec(one_slab, lambda i: (base // block + i, 0, 0, 0))

    def plane_at(base):
        return pl.BlockSpec(one_plane, lambda i: (base // block + i, 0, 0))

    def call(kernel, piece, fresh, in_specs, args, out_specs, out_shape, alias):
        elements = size * planes * rows * columns
        return pl.pallas_call(
            functools.partial(kernel, piece * size, planes, coupling, fresh),
            grid=(size // block,),
            in_specs=[scalar] * 3 + in_specs,
            out_specs=out_specs,
            out_shape=out_shape,
            input_output_aliases=alias,
            cost_estimate=pl.CostEstimate(flops=WORK * elements, bytes_accessed=BYTES * elements, transcendentals=0),
            compiler_params=pltpu.CompilerParams(
                dimension_semantics=("arbitrary",), vmem_limit_bytes=32 * 1024 * 1024
            ),
        )(odd_arr, mobility, stiffness, *args)

    far, sums_at = [], []

    def field_piece(index):
        array = initial if index < count else cotangent
        return cut(array, far_plane, (index % count) * size, size)

    def start_until(limit):
        while len(far) < min(limit, 2 * count):
            index = len(far)
            piece = field_piece(index) if index else first
            before = []
            if index >= IN_FLIGHT:
                before.append(far[index - IN_FLIGHT])
            if index > IN_FLIGHT and len(sums_at) > index - IN_FLIGHT - 1:
                before.append(sums_at[index - IN_FLIGHT - 1])
            far.append(send_far(after(piece, *before)))

    first = cut(initial, far_plane, 0, size)
    squares_first = order_sum(jnp.sum(initial * initial, 0))
    near_share = NEAR_SHARE if count % NEAR_SHARE == 0 else 1
    near = []

    def near_until(index):
        while len(near) * near_share <= index:
            piece = len(near) * near_share
            array = initial if piece < count else cotangent
            plane = cut(array, near_plane, (piece % count) * size, near_share * size)
            before = [far[piece - NEAR_LAG]] if piece >= NEAR_LAG else ([first] if FIRST else [])
            near.append(send_near(after(plane, *before)))

    start_until(IN_FLIGHT)

    middle, sums = [], None
    for k in range(count):
        start_until(IN_FLIGHT + k)
        near_until(k)
        fresh = k == 0
        value, sums = call(
            middle_kernel, k, fresh,
            [slab_at(k * size), slab_at(k * size), plane_at(0), plane_at((k % near_share) * size), cell_spec]
            + ([] if fresh else [cells_spec]),
            [initial, cotangent, far[k], near[k // near_share], squares_first] + ([] if fresh else [sums]),
            [slab_at(0), cells_spec], [slab, cells], {} if fresh else {8: 1},
        )
        middle.append(value)
        sums_at.append(sums)
    start_until(2 * count)
    near_until(2 * count - 1)
    sums = order_sum(sums)

    outs, coupled, held = [], None, None
    back, back_near, helds = [], [], []
    share = BACK_SHARE if count % BACK_SHARE == 0 else 1
    for k in range(count):
        fresh, inside = k == 0, (k % share) * size
        specs = [slab_at(k * size), slab_at(0), slab_at(k * size), plane_at(0), plane_at((k % near_share) * size), cells_spec]
        args = [initial, middle[k], cotangent, far[count + k], near[(count + k) // near_share], sums]
        if BACK and k >= BACK and k - BACK < len(back):
            args[1] = after(middle[k], back[k - BACK])
        alias = {}
        if not fresh:
            specs, args = specs + [cell_spec], args + [coupled]
            alias[3 + len(args) - 1] = planes
        if k % share:
            for position in range(1, planes):
                specs, args = specs + [anywhere], args + [held[position - 1]]
                alias[3 + len(args) - 1] = position
        outer, *held, coupled = call(
            adjoint_kernel, k, fresh, specs, args,
            [plane_at(0)] + [plane_at(inside)] * (planes - 1) + [cell_spec],
            [plane_out] + [shape(share * size, rows, columns)] * (planes - 1) + [cell], alias,
        )
        outs.append(outer)
        if k <= AHEAD:
            back.append(send_far(outer))
        if (k + 1) % share == 0:
            plane = held[-1]
            if BACK_LAG and k >= BACK_LAG:
                plane = after(plane, back[min(k - BACK_LAG, len(back) - 1)])
            back_near.append(send_near(plane))
            helds.append(held)
    coupled = order_sum(coupled)

    result = None
    for k in range(count):
        fresh, inside = k == 0, (k % share) * size
        result, token = call(
            last_kernel, k, fresh,
            [slab_at(k * size), plane_at(0), plane_at(inside), cell_spec, cell_spec, plane_at(0)]
            + [plane_at(inside)] * (planes - 1) + ([] if fresh else [anywhere]),
            [initial, back[k], back_near[k // share], squares_first, coupled, outs[k]] + helds[k // share]
            + ([] if fresh else [result]),
            [slab_at(k * size), pl.BlockSpec((8, 128), lambda i: (0, 0))],
            [shape(*initial.shape), shape(8, 128)], {} if fresh else {8 + planes: 0},
        )
        if len(back) < count:
            back.append(send_far(after(outs[len(back)], back[k + 1], token)))
    return result


def solution(mesh):
    return jax.shard_map(
        on_device,
        mesh=mesh,
        in_specs=(P("ord", "gz", None, None), P("ord", "gz", None, None), P("ord"), P("ord")),
        out_specs=P("ord", "gz", None, None),
        check_vma=False,
    )
```

```python
import functools
import math

import jax
import jax.numpy as jnp
from jax import lax
from jax.experimental import pallas as pl
from jax.experimental.pallas import tpu as pltpu
from jax.sharding import PartitionSpec as P

couple_scale = 2.0
PIECES = 6
IN_FLIGHT = 3
STEP_ORDERS = 4
WORK = 30
BYTES = 20
BACK = 0
NEAR_SHARE = 1
NEAR_LAG = 16
FIRST = True
BACK_GROUPS = (1, 1, 1, 1, 1, 1)
AHEAD = 4
CARRY = True
EARLY = True
FAR_FIRST = 2


def pieces_of(orders):
    count = min(PIECES, orders)
    while orders % count:
        count -= 1
    return count, orders // count


def inner_pairs(count):
    return [(i, i ^ 1) for i in range(count)]


def outer_pairs(count):
    return [(i, (i + 1) % count if i % 2 else (i - 1) % count) for i in range(count)]


def order_sum(values):
    count = lax.axis_size("ord")
    if count & (count - 1):
        return lax.psum(values, "ord")
    step = 1
    while step < count:
        values = values + lax.ppermute(values, "ord", [(i, i ^ step) for i in range(count)])
        step *= 2
    return values


def in_plane(plane):
    rows, columns = plane.shape
    return (
        pltpu.roll(plane, 1, 0)
        + pltpu.roll(plane, rows - 1, 0)
        + pltpu.roll(plane, 1, 1)
        + pltpu.roll(plane, columns - 1, 1)
    )


def place(odd, position, planes):
    return position + odd * (planes - 1 - 2 * position)


def middle_kernel(base, planes, coupling, fresh, odd_ref, rate_ref, stiff_ref, field, adjoint, far, near, squares, *rest):
    if fresh:
        middle, sums = rest
    else:
        sums_before, middle, sums = rest
    step = pl.program_id(0)
    block = field.shape[0]
    odd = odd_ref[0]

    @pl.when(step == 0)
    def _():
        sums[...] = jnp.zeros_like(sums) if fresh else sums_before[...]

    for position in range(planes):
        z = place(odd, position, planes)
        squared, coupled = sums[0, z], sums[1, z]
        scaled_squares = (2.0 * coupling) * squares[z]
        for p in range(block):
            rate = rate_ref[base + step * block + p]
            stiff = rate * stiff_ref[base + step * block + p]
            centre = field[p, z]
            before = far[p] if position == 0 else field[p, place(odd, position - 1, planes)]
            after = near[p] if position == planes - 1 else field[p, place(odd, position + 1, planes)]
            around = in_plane(centre) + (before + after)
            factor = (1.0 + rate - 6.0 * stiff) - rate * (
                scaled_squares + (1.0 - 2.0 * coupling) * (centre * centre)
            )
            value = centre * factor + stiff * around
            middle[p, z] = value
            squared = squared + value * value
            coupled = coupled + value * (rate * adjoint[p, z])
        sums[0, z] = squared
        sums[1, z] = coupled


def pulled_back(rate, stiff, coupling, value, adjoint, around, squares, coupled):
    factor = (1.0 + rate - 6.0 * stiff) - rate * (squares + (3.0 - 6.0 * coupling) * (value * value))
    return adjoint * factor - value * coupled + stiff * around


def adjoint_kernel(base, planes, coupling, fresh, odd_ref, rate_ref, stiff_ref, field, middle, adjoint, far, near, squares, sums, *rest):
    outer, inner, own, coupled = rest[-4:]
    step = pl.program_id(0)
    block = field.shape[0]
    odd = odd_ref[0]

    @pl.when(step == 0)
    def _():
        coupled[...] = jnp.zeros_like(coupled) if fresh else rest[0][...]

    zs = [place(odd, position, planes) for position in range(planes)]
    totals = [coupled[z] for z in zs]
    for p in range(block):
        rate = rate_ref[base + step * block + p]
        stiff = rate * stiff_ref[base + step * block + p]
        values = []
        for position, z in enumerate(zs):
            centre = adjoint[p, z]
            before = far[p] if position == 0 else adjoint[p, zs[position - 1]]
            after = near[p] if position == planes - 1 else adjoint[p, zs[position + 1]]
            around = in_plane(centre) + (before + after)
            value = pulled_back(
                rate, stiff, coupling, middle[p, z], centre, around,
                (2.0 * coupling) * sums[0, z], (4.0 * coupling) * sums[1, z],
            )
            values.append(value)
            totals[position] = totals[position] + field[p, z] * (rate * value)
        outer[p] = values[0]
        inner[p] = values[-1]
        for position, z in enumerate(zs):
            around = in_plane(values[position])
            if position > 0:
                around = around + values[position - 1]
            if position < planes - 1:
                around = around + values[position + 1]
            square = field[p, z] * field[p, z]
            factor = (1.0 + rate - 6.0 * stiff) - rate * (
                (2.0 * coupling) * squares[z] + (3.0 - 6.0 * coupling) * square
            )
            own[p, z] = values[position] * factor + stiff * around
    for position, z in enumerate(zs):
        coupled[z] = totals[position]


def last_kernel(base, planes, coupling, fresh, odd_ref, rate_ref, stiff_ref, field, far, near, coupled, own, *rest):
    out = rest[-1] if rest[-1].shape == field.shape else rest[-2]
    step = pl.program_id(0)
    block = field.shape[0]
    odd = odd_ref[0]
    for position in range(planes):
        z = place(odd, position, planes)
        pull = (4.0 * coupling) * coupled[z]
        for p in range(block):
            rate = rate_ref[base + step * block + p]
            stiff = rate * stiff_ref[base + step * block + p]
            value = own[p, z] - field[p, z] * pull
            if position == 0:
                value = value + stiff * far[p]
            if position == planes - 1:
                value = value + stiff * near[p]
            out[p, z] = value


def on_device(initial, cotangent, mobility, stiffness):
    orders, planes, rows, columns = initial.shape
    coupling = couple_scale / (orders * lax.axis_size("ord"))
    count, size = pieces_of(orders)
    joined = min(FAR_FIRST, count)
    block = math.gcd(size, STEP_ORDERS)
    ring = lax.axis_size("gz")
    odd = lax.rem(lax.axis_index("gz"), 2)
    odd_arr = odd.reshape(1).astype(jnp.int32)
    far_plane = odd * (planes - 1)
    near_plane = (planes - 1) - far_plane

    def send_far(plane):
        return lax.ppermute(plane, "gz", outer_pairs(ring))

    def send_near(plane):
        return lax.ppermute(plane, "gz", inner_pairs(ring))

    def cut(array, plane, start, length):
        return lax.dynamic_slice(array, (start, plane, 0, 0), (length, 1, rows, columns)).reshape(length, rows, columns)

    def after(value, *before):
        return lax.optimization_barrier((value, before))[0] if before else value

    scalar = pl.BlockSpec(memory_space=pltpu.SMEM)
    anywhere = pl.BlockSpec(memory_space=pl.ANY)
    one_slab = (block, planes, rows, columns)
    one_plane = (block, rows, columns)

    def shape(*dims):
        return jax.ShapeDtypeStruct(dims, jnp.float32)

    slab = shape(size, planes, rows, columns)
    plane_out = shape(size, rows, columns)
    cell = shape(planes, rows, columns)
    cells = shape(2, planes, rows, columns)
    cell_spec = pl.BlockSpec(cell.shape, lambda i: (0, 0, 0))
    cells_spec = pl.BlockSpec(cells.shape, lambda i: (0, 0, 0, 0))

    def slab_at(base):
        return pl.BlockSpec(one_slab, lambda i: (base // block + i, 0, 0, 0))

    def plane_at(base):
        return pl.BlockSpec(one_plane, lambda i: (base // block + i, 0, 0))

    def call(kernel, piece, fresh, in_specs, args, out_specs, out_shape, alias, tokens=()):
        elements = size * planes * rows * columns
        return pl.pallas_call(
            functools.partial(kernel, piece * size, planes, coupling, fresh),
            grid=(size // block,),
            in_specs=[scalar] * 3 + in_specs + [anywhere] * len(tokens),
            out_specs=out_specs,
            out_shape=out_shape,
            input_output_aliases=alias,
            cost_estimate=pl.CostEstimate(flops=WORK * elements, bytes_accessed=BYTES * elements, transcendentals=0),
            compiler_params=pltpu.CompilerParams(
                dimension_semantics=("arbitrary",), vmem_limit_bytes=32 * 1024 * 1024
            ),
        )(odd_arr, mobility, stiffness, *args, *tokens)

    far, sums_at = [], []

    def field_piece(index):
        array = initial if index < count else cotangent
        return cut(array, far_plane, (index % count) * size, size)

    def start_until(limit):
        while len(far) < min(limit, 2 * count):
            index = len(far)
            piece = field_piece(index) if index else first
            before = []
            if index >= IN_FLIGHT:
                before.append(far[index - IN_FLIGHT])
            if index > IN_FLIGHT and len(sums_at) > index - IN_FLIGHT - 1:
                before.append(sums_at[index - IN_FLIGHT - 1])
            sent = send_far(after(piece, *before))
            far.extend([sent] * (joined if index == 0 else 1))

    first = cut(initial, far_plane, 0, joined * size)
    squares_first = order_sum(jnp.sum(initial * initial, 0))
    near_share = NEAR_SHARE if count % NEAR_SHARE == 0 else 1
    near = []

    def near_until(index):
        while len(near) * near_share <= index:
            piece = len(near) * near_share
            array = initial if piece < count else cotangent
            plane = cut(array, near_plane, (piece % count) * size, near_share * size)
            before = [far[piece - NEAR_LAG]] if piece >= NEAR_LAG else ([first] if FIRST else [])
            near.append(send_near(after(plane, *before)))

    start_until(IN_FLIGHT)
    if EARLY:
        near_until(2 * count - 1)

    middle, sums = [], None
    for k in range(count):
        start_until(IN_FLIGHT + k)
        near_until(k)
        fresh = k == 0
        value, sums = call(
            middle_kernel, k, fresh,
            [slab_at(k * size), slab_at(k * size), plane_at(k * size if k < joined else 0),
             plane_at((k % near_share) * size), cell_spec]
            + ([] if fresh else [cells_spec]),
            [initial, cotangent, far[k], near[k // near_share], squares_first] + ([] if fresh else [sums]),
            [slab_at(0), cells_spec], [slab, cells], {} if fresh else {8: 1},
        )
        middle.append(value)
        sums_at.append(sums)
    start_until(2 * count)
    near_until(2 * count - 1)
    sums = order_sum(sums)

    outs, coupled, held = [], None, None
    back, back_near, owns = [], [], []
    groups = BACK_GROUPS if sum(BACK_GROUPS) == count else (1,) * count
    opens = [sum(groups[:g]) for g in range(len(groups))]
    group_of = [g for g, members in enumerate(groups) for _ in range(members)]
    for k in range(count):
        fresh, group = k == 0, group_of[k]
        inside = (k - opens[group]) * size
        specs = [slab_at(k * size), slab_at(0), slab_at(k * size), plane_at(0), plane_at((k % near_share) * size), cell_spec, cells_spec]
        args = [initial, middle[k], cotangent, far[count + k], near[(count + k) // near_share], squares_first, sums]
        tokens = []
        if BACK and k >= BACK and k - BACK < len(back):
            tokens = [back[k - BACK]]
        alias = {}
        if not fresh:
            specs, args = specs + [cell_spec], args + [coupled]
            alias[3 + len(args) - 1] = 3
        if k != opens[group]:
            specs, args = specs + [anywhere], args + [held]
            alias[3 + len(args) - 1] = 1
        outer, held, own, coupled = call(
            adjoint_kernel, k, fresh, specs, args,
            [plane_at(0), plane_at(inside), slab_at(0), cell_spec],
            [plane_out, shape(groups[group] * size, rows, columns), slab, cell], alias, tokens,
        )
        owns.append(own)
        outs.append(outer)
        if k <= AHEAD or not CARRY:
            back.append(send_far(outer))
        if k + 1 == opens[group] + groups[group]:
            plane = held
            back_near.append(send_near(plane))
    coupled = order_sum(coupled)

    result = None
    for k in range(count):
        fresh, group = k == 0, group_of[k]
        inside = (k - opens[group]) * size
        later = len(back) if CARRY and len(back) < count else None
        specs = [slab_at(k * size), plane_at(0), plane_at(inside), cell_spec, slab_at(0)]
        args = [initial, back[k], back_near[group], coupled, owns[k]]
        out_specs, out_shape, alias = [slab_at(k * size)], [shape(*initial.shape)], {}
        if not fresh:
            specs, args = specs + [anywhere], args + [result]
            alias[3 + len(args) - 1] = 0
        if later is not None:
            specs, args = specs + [anywhere], args + [outs[later]]
            out_specs, out_shape = out_specs + [anywhere], out_shape + [plane_out]
            alias[3 + len(args) - 1] = 1
        result, *handed = call(last_kernel, k, fresh, specs, args, out_specs, out_shape, alias)
        if later is not None:
            back.append(send_far(handed[0]))
    return result


def solution(mesh):
    return jax.shard_map(
        on_device,
        mesh=mesh,
        in_specs=(P("ord", "gz", None, None), P("ord", "gz", None, None), P("ord"), P("ord")),
        out_specs=P("ord", "gz", None, None),
        check_vma=False,
    )
```

```python
import functools
import math

import jax
import jax.numpy as jnp
from jax import lax
from jax.experimental import pallas as pl
from jax.experimental.pallas import tpu as pltpu
from jax.sharding import PartitionSpec as P

couple_scale = 2.0
PIECES = 6
IN_FLIGHT = 3
STEP_ORDERS = 4
WORK = 30
BYTES = 20
BACK = 0
NEAR_SHARE = 1
NEAR_LAG = 16
FIRST = True
BACK_GROUPS = (1, 1, 1, 1, 1, 1)
AHEAD = 3
CARRY = True
EARLY = True
FAR_FIRST = 2


def pieces_of(orders):
    count = min(PIECES, orders)
    while orders % count:
        count -= 1
    return count, orders // count


def inner_pairs(count):
    return [(i, i ^ 1) for i in range(count)]


def outer_pairs(count):
    return [(i, (i + 1) % count if i % 2 else (i - 1) % count) for i in range(count)]


def order_sum(values):
    count = lax.axis_size("ord")
    if count & (count - 1):
        return lax.psum(values, "ord")
    step = 1
    while step < count:
        values = values + lax.ppermute(values, "ord", [(i, i ^ step) for i in range(count)])
        step *= 2
    return values


def in_plane(plane):
    rows, columns = plane.shape
    return (
        pltpu.roll(plane, 1, 0)
        + pltpu.roll(plane, rows - 1, 0)
        + pltpu.roll(plane, 1, 1)
        + pltpu.roll(plane, columns - 1, 1)
    )


def place(odd, position, planes):
    return position + odd * (planes - 1 - 2 * position)


def middle_kernel(base, planes, coupling, fresh, odd_ref, rate_ref, stiff_ref, field, adjoint, far, near, squares, *rest):
    if fresh:
        middle, sums = rest
    else:
        sums_before, middle, sums = rest
    step = pl.program_id(0)
    block = field.shape[0]
    odd = odd_ref[0]

    @pl.when(step == 0)
    def _():
        sums[...] = jnp.zeros_like(sums) if fresh else sums_before[...]

    for position in range(planes):
        z = place(odd, position, planes)
        squared, coupled = sums[0, z], sums[1, z]
        scaled_squares = (2.0 * coupling) * squares[z]
        for p in range(block):
            rate = rate_ref[base + step * block + p]
            stiff = rate * stiff_ref[base + step * block + p]
            centre = field[p, z]
            before = far[p] if position == 0 else field[p, place(odd, position - 1, planes)]
            after = near[p] if position == planes - 1 else field[p, place(odd, position + 1, planes)]
            around = in_plane(centre) + (before + after)
            factor = (1.0 + rate - 6.0 * stiff) - rate * (
                scaled_squares + (1.0 - 2.0 * coupling) * (centre * centre)
            )
            value = centre * factor + stiff * around
            middle[p, z] = value
            squared = squared + value * value
            coupled = coupled + value * (rate * adjoint[p, z])
        sums[0, z] = squared
        sums[1, z] = coupled


def pulled_back(rate, stiff, coupling, value, adjoint, around, squares, coupled):
    factor = (1.0 + rate - 6.0 * stiff) - rate * (squares + (3.0 - 6.0 * coupling) * (value * value))
    return adjoint * factor - value * coupled + stiff * around


def adjoint_kernel(base, planes, coupling, fresh, odd_ref, rate_ref, stiff_ref, field, middle, adjoint, far, near, squares, sums, *rest):
    outer, inner, own, coupled = rest[-4:]
    step = pl.program_id(0)
    block = field.shape[0]
    odd = odd_ref[0]

    @pl.when(step == 0)
    def _():
        coupled[...] = jnp.zeros_like(coupled) if fresh else rest[0][...]

    zs = [place(odd, position, planes) for position in range(planes)]
    totals = [coupled[z] for z in zs]
    for p in range(block):
        rate = rate_ref[base + step * block + p]
        stiff = rate * stiff_ref[base + step * block + p]
        values = []
        for position, z in enumerate(zs):
            centre = adjoint[p, z]
            before = far[p] if position == 0 else adjoint[p, zs[position - 1]]
            after = near[p] if position == planes - 1 else adjoint[p, zs[position + 1]]
            around = in_plane(centre) + (before + after)
            value = pulled_back(
                rate, stiff, coupling, middle[p, z], centre, around,
                (2.0 * coupling) * sums[0, z], (4.0 * coupling) * sums[1, z],
            )
            values.append(value)
            totals[position] = totals[position] + field[p, z] * (rate * value)
        outer[p] = values[0]
        inner[p] = values[-1]
        for position, z in enumerate(zs):
            around = in_plane(values[position])
            if position > 0:
                around = around + values[position - 1]
            if position < planes - 1:
                around = around + values[position + 1]
            square = field[p, z] * field[p, z]
            factor = (1.0 + rate - 6.0 * stiff) - rate * (
                (2.0 * coupling) * squares[z] + (3.0 - 6.0 * coupling) * square
            )
            own[p, z] = values[position] * factor + stiff * around
    for position, z in enumerate(zs):
        coupled[z] = totals[position]


def last_kernel(base, planes, coupling, fresh, odd_ref, rate_ref, stiff_ref, field, far, near, coupled, own, *rest):
    out = rest[-1] if rest[-1].shape == field.shape else rest[-2]
    step = pl.program_id(0)
    block = field.shape[0]
    odd = odd_ref[0]
    for position in range(planes):
        z = place(odd, position, planes)
        pull = (4.0 * coupling) * coupled[z]
        for p in range(block):
            rate = rate_ref[base + step * block + p]
            stiff = rate * stiff_ref[base + step * block + p]
            value = own[p, z] - field[p, z] * pull
            if position == 0:
                value = value + stiff * far[p]
            if position == planes - 1:
                value = value + stiff * near[p]
            out[p, z] = value


def on_device(initial, cotangent, mobility, stiffness):
    orders, planes, rows, columns = initial.shape
    coupling = couple_scale / (orders * lax.axis_size("ord"))
    count, size = pieces_of(orders)
    joined = min(FAR_FIRST, count)
    block = math.gcd(size, STEP_ORDERS)
    ring = lax.axis_size("gz")
    odd = lax.rem(lax.axis_index("gz"), 2)
    odd_arr = odd.reshape(1).astype(jnp.int32)
    far_plane = odd * (planes - 1)
    near_plane = (planes - 1) - far_plane

    def send_far(plane):
        return lax.ppermute(plane, "gz", outer_pairs(ring))

    def send_near(plane):
        return lax.ppermute(plane, "gz", inner_pairs(ring))

    def cut(array, plane, start, length):
        return lax.dynamic_slice(array, (start, plane, 0, 0), (length, 1, rows, columns)).reshape(length, rows, columns)

    def after(value, *before):
        return lax.optimization_barrier((value, before))[0] if before else value

    scalar = pl.BlockSpec(memory_space=pltpu.SMEM)
    anywhere = pl.BlockSpec(memory_space=pl.ANY)
    one_slab = (block, planes, rows, columns)
    one_plane = (block, rows, columns)

    def shape(*dims):
        return jax.ShapeDtypeStruct(dims, jnp.float32)

    slab = shape(size, planes, rows, columns)
    plane_out = shape(size, rows, columns)
    cell = shape(planes, rows, columns)
    cells = shape(2, planes, rows, columns)
    cell_spec = pl.BlockSpec(cell.shape, lambda i: (0, 0, 0))
    cells_spec = pl.BlockSpec(cells.shape, lambda i: (0, 0, 0, 0))

    def slab_at(base):
        return pl.BlockSpec(one_slab, lambda i: (base // block + i, 0, 0, 0))

    def plane_at(base):
        return pl.BlockSpec(one_plane, lambda i: (base // block + i, 0, 0))

    def call(kernel, piece, fresh, in_specs, args, out_specs, out_shape, alias, tokens=()):
        elements = size * planes * rows * columns
        return pl.pallas_call(
            functools.partial(kernel, piece * size, planes, coupling, fresh),
            grid=(size // block,),
            in_specs=[scalar] * 3 + in_specs + [anywhere] * len(tokens),
            out_specs=out_specs,
            out_shape=out_shape,
            input_output_aliases=alias,
            cost_estimate=pl.CostEstimate(flops=WORK * elements, bytes_accessed=BYTES * elements, transcendentals=0),
            compiler_params=pltpu.CompilerParams(
                dimension_semantics=("arbitrary",), vmem_limit_bytes=32 * 1024 * 1024
            ),
        )(odd_arr, mobility, stiffness, *args, *tokens)

    far, sums_at = [], []

    def field_piece(index):
        array = initial if index < count else cotangent
        return cut(array, far_plane, (index % count) * size, size)

    def start_until(limit):
        while len(far) < min(limit, 2 * count):
            index = len(far)
            piece = field_piece(index) if index else first
            before = []
            if index >= IN_FLIGHT:
                before.append(far[index - IN_FLIGHT])
            if index > IN_FLIGHT and len(sums_at) > index - IN_FLIGHT - 1:
                before.append(sums_at[index - IN_FLIGHT - 1])
            sent = send_far(after(piece, *before))
            far.extend([sent] * (joined if index == 0 else 1))

    first = cut(initial, far_plane, 0, joined * size)
    squares_first = order_sum(jnp.sum(initial * initial, 0))
    near_share = NEAR_SHARE if count % NEAR_SHARE == 0 else 1
    near = []

    def near_until(index):
        while len(near) * near_share <= index:
            piece = len(near) * near_share
            array = initial if piece < count else cotangent
            plane = cut(array, near_plane, (piece % count) * size, near_share * size)
            before = [far[piece - NEAR_LAG]] if piece >= NEAR_LAG else ([first] if FIRST else [])
            near.append(send_near(after(plane, *before)))

    start_until(IN_FLIGHT)
    if EARLY:
        near_until(2 * count - 1)

    middle, sums = [], None
    for k in range(count):
        start_until(IN_FLIGHT + k)
        near_until(k)
        fresh = k == 0
        value, sums = call(
            middle_kernel, k, fresh,
            [slab_at(k * size), slab_at(k * size), plane_at(k * size if k < joined else 0),
             plane_at((k % near_share) * size), cell_spec]
            + ([] if fresh else [cells_spec]),
            [initial, cotangent, far[k], near[k // near_share], squares_first] + ([] if fresh else [sums]),
            [slab_at(0), cells_spec], [slab, cells], {} if fresh else {8: 1},
        )
        middle.append(value)
        sums_at.append(sums)
    start_until(2 * count)
    near_until(2 * count - 1)
    sums = order_sum(sums)

    outs, coupled, held = [], None, None
    back, back_near, owns = [], [], []
    groups = BACK_GROUPS if sum(BACK_GROUPS) == count else (1,) * count
    opens = [sum(groups[:g]) for g in range(len(groups))]
    group_of = [g for g, members in enumerate(groups) for _ in range(members)]
    for k in range(count):
        fresh, group = k == 0, group_of[k]
        inside = (k - opens[group]) * size
        specs = [slab_at(k * size), slab_at(0), slab_at(k * size), plane_at(0), plane_at((k % near_share) * size), cell_spec, cells_spec]
        args = [initial, middle[k], cotangent, far[count + k], near[(count + k) // near_share], squares_first, sums]
        tokens = []
        if BACK and k >= BACK and k - BACK < len(back):
            tokens = [back[k - BACK]]
        alias = {}
        if not fresh:
            specs, args = specs + [cell_spec], args + [coupled]
            alias[3 + len(args) - 1] = 3
        if k != opens[group]:
            specs, args = specs + [anywhere], args + [held]
            alias[3 + len(args) - 1] = 1
        outer, held, own, coupled = call(
            adjoint_kernel, k, fresh, specs, args,
            [plane_at(0), plane_at(inside), slab_at(0), cell_spec],
            [plane_out, shape(groups[group] * size, rows, columns), slab, cell], alias, tokens,
        )
        owns.append(own)
        outs.append(outer)
        if k <= AHEAD or not CARRY:
            back.append(send_far(outer))
        if k + 1 == opens[group] + groups[group]:
            plane = held
            back_near.append(send_near(plane))
    coupled = order_sum(coupled)

    result = None
    for k in range(count):
        fresh, group = k == 0, group_of[k]
        inside = (k - opens[group]) * size
        later = len(back) if CARRY and len(back) < count else None
        specs = [slab_at(k * size), plane_at(0), plane_at(inside), cell_spec, slab_at(0)]
        args = [initial, back[k], back_near[group], coupled, owns[k]]
        out_specs, out_shape, alias = [slab_at(k * size)], [shape(*initial.shape)], {}
        if not fresh:
            specs, args = specs + [anywhere], args + [result]
            alias[3 + len(args) - 1] = 0
        if later is not None:
            specs, args = specs + [anywhere], args + [outs[later]]
            out_specs, out_shape = out_specs + [anywhere], out_shape + [plane_out]
            alias[3 + len(args) - 1] = 1
        result, *handed = call(last_kernel, k, fresh, specs, args, out_specs, out_shape, alias)
        if later is not None:
            back.append(send_far(handed[0]))
    return result


def solution(mesh):
    return jax.shard_map(
        on_device,
        mesh=mesh,
        in_specs=(P("ord", "gz", None, None), P("ord", "gz", None, None), P("ord"), P("ord")),
        out_specs=P("ord", "gz", None, None),
        check_vma=False,
    )
```

```python
import functools
import math

import jax
import jax.numpy as jnp
from jax import lax
from jax.experimental import pallas as pl
from jax.experimental.pallas import tpu as pltpu
from jax.sharding import PartitionSpec as P

couple_scale = 2.0
PIECES = 6
IN_FLIGHT = 3
STEP_ORDERS = 4
WORK = 30
BYTES = 20
BACK = 0
NEAR_SHARE = 1
NEAR_LAG = 16
FIRST = True
BACK_GROUPS = (1, 1, 1, 1, 1, 1)
AHEAD = 2
CARRY = True
EARLY = True
FAR_FIRST = 2


def pieces_of(orders):
    count = min(PIECES, orders)
    while orders % count:
        count -= 1
    return count, orders // count


def inner_pairs(count):
    return [(i, i ^ 1) for i in range(count)]


def outer_pairs(count):
    return [(i, (i + 1) % count if i % 2 else (i - 1) % count) for i in range(count)]


def order_sum(values):
    count = lax.axis_size("ord")
    if count & (count - 1):
        return lax.psum(values, "ord")
    step = 1
    while step < count:
        values = values + lax.ppermute(values, "ord", [(i, i ^ step) for i in range(count)])
        step *= 2
    return values


def in_plane(plane):
    rows, columns = plane.shape
    return (
        pltpu.roll(plane, 1, 0)
        + pltpu.roll(plane, rows - 1, 0)
        + pltpu.roll(plane, 1, 1)
        + pltpu.roll(plane, columns - 1, 1)
    )


def place(odd, position, planes):
    return position + odd * (planes - 1 - 2 * position)


def middle_kernel(base, planes, coupling, fresh, odd_ref, rate_ref, stiff_ref, field, adjoint, far, near, squares, *rest):
    if fresh:
        middle, sums = rest
    else:
        sums_before, middle, sums = rest
    step = pl.program_id(0)
    block = field.shape[0]
    odd = odd_ref[0]

    @pl.when(step == 0)
    def _():
        sums[...] = jnp.zeros_like(sums) if fresh else sums_before[...]

    for position in range(planes):
        z = place(odd, position, planes)
        squared, coupled = sums[0, z], sums[1, z]
        scaled_squares = (2.0 * coupling) * squares[z]
        for p in range(block):
            rate = rate_ref[base + step * block + p]
            stiff = rate * stiff_ref[base + step * block + p]
            centre = field[p, z]
            before = far[p] if position == 0 else field[p, place(odd, position - 1, planes)]
            after = near[p] if position == planes - 1 else field[p, place(odd, position + 1, planes)]
            around = in_plane(centre) + (before + after)
            factor = (1.0 + rate - 6.0 * stiff) - rate * (
                scaled_squares + (1.0 - 2.0 * coupling) * (centre * centre)
            )
            value = centre * factor + stiff * around
            middle[p, z] = value
            squared = squared + value * value
            coupled = coupled + value * (rate * adjoint[p, z])
        sums[0, z] = squared
        sums[1, z] = coupled


def pulled_back(rate, stiff, coupling, value, adjoint, around, squares, coupled):
    factor = (1.0 + rate - 6.0 * stiff) - rate * (squares + (3.0 - 6.0 * coupling) * (value * value))
    return adjoint * factor - value * coupled + stiff * around


def adjoint_kernel(base, planes, coupling, fresh, odd_ref, rate_ref, stiff_ref, field, middle, adjoint, far, near, squares, sums, *rest):
    outer, inner, own, coupled = rest[-4:]
    step = pl.program_id(0)
    block = field.shape[0]
    odd = odd_ref[0]

    @pl.when(step == 0)
    def _():
        coupled[...] = jnp.zeros_like(coupled) if fresh else rest[0][...]

    zs = [place(odd, position, planes) for position in range(planes)]
    totals = [coupled[z] for z in zs]
    for p in range(block):
        rate = rate_ref[base + step * block + p]
        stiff = rate * stiff_ref[base + step * block + p]
        values = []
        for position, z in enumerate(zs):
            centre = adjoint[p, z]
            before = far[p] if position == 0 else adjoint[p, zs[position - 1]]
            after = near[p] if position == planes - 1 else adjoint[p, zs[position + 1]]
            around = in_plane(centre) + (before + after)
            value = pulled_back(
                rate, stiff, coupling, middle[p, z], centre, around,
                (2.0 * coupling) * sums[0, z], (4.0 * coupling) * sums[1, z],
            )
            values.append(value)
            totals[position] = totals[position] + field[p, z] * (rate * value)
        outer[p] = values[0]
        inner[p] = values[-1]
        for position, z in enumerate(zs):
            around = in_plane(values[position])
            if position > 0:
                around = around + values[position - 1]
            if position < planes - 1:
                around = around + values[position + 1]
            square = field[p, z] * field[p, z]
            factor = (1.0 + rate - 6.0 * stiff) - rate * (
                (2.0 * coupling) * squares[z] + (3.0 - 6.0 * coupling) * square
            )
            own[p, z] = values[position] * factor + stiff * around
    for position, z in enumerate(zs):
        coupled[z] = totals[position]


def last_kernel(base, planes, coupling, fresh, odd_ref, rate_ref, stiff_ref, field, far, near, coupled, own, *rest):
    out = rest[-1] if rest[-1].shape == field.shape else rest[-2]
    step = pl.program_id(0)
    block = field.shape[0]
    odd = odd_ref[0]
    for position in range(planes):
        z = place(odd, position, planes)
        pull = (4.0 * coupling) * coupled[z]
        for p in range(block):
            rate = rate_ref[base + step * block + p]
            stiff = rate * stiff_ref[base + step * block + p]
            value = own[p, z] - field[p, z] * pull
            if position == 0:
                value = value + stiff * far[p]
            if position == planes - 1:
                value = value + stiff * near[p]
            out[p, z] = value


def on_device(initial, cotangent, mobility, stiffness):
    orders, planes, rows, columns = initial.shape
    coupling = couple_scale / (orders * lax.axis_size("ord"))
    count, size = pieces_of(orders)
    joined = min(FAR_FIRST, count)
    block = math.gcd(size, STEP_ORDERS)
    ring = lax.axis_size("gz")
    odd = lax.rem(lax.axis_index("gz"), 2)
    odd_arr = odd.reshape(1).astype(jnp.int32)
    far_plane = odd * (planes - 1)
    near_plane = (planes - 1) - far_plane

    def send_far(plane):
        return lax.ppermute(plane, "gz", outer_pairs(ring))

    def send_near(plane):
        return lax.ppermute(plane, "gz", inner_pairs(ring))

    def cut(array, plane, start, length):
        return lax.dynamic_slice(array, (start, plane, 0, 0), (length, 1, rows, columns)).reshape(length, rows, columns)

    def after(value, *before):
        return lax.optimization_barrier((value, before))[0] if before else value

    scalar = pl.BlockSpec(memory_space=pltpu.SMEM)
    anywhere = pl.BlockSpec(memory_space=pl.ANY)
    one_slab = (block, planes, rows, columns)
    one_plane = (block, rows, columns)

    def shape(*dims):
        return jax.ShapeDtypeStruct(dims, jnp.float32)

    slab = shape(size, planes, rows, columns)
    plane_out = shape(size, rows, columns)
    cell = shape(planes, rows, columns)
    cells = shape(2, planes, rows, columns)
    cell_spec = pl.BlockSpec(cell.shape, lambda i: (0, 0, 0))
    cells_spec = pl.BlockSpec(cells.shape, lambda i: (0, 0, 0, 0))

    def slab_at(base):
        return pl.BlockSpec(one_slab, lambda i: (base // block + i, 0, 0, 0))

    def plane_at(base):
        return pl.BlockSpec(one_plane, lambda i: (base // block + i, 0, 0))

    def call(kernel, piece, fresh, in_specs, args, out_specs, out_shape, alias, tokens=()):
        elements = size * planes * rows * columns
        return pl.pallas_call(
            functools.partial(kernel, piece * size, planes, coupling, fresh),
            grid=(size // block,),
            in_specs=[scalar] * 3 + in_specs + [anywhere] * len(tokens),
            out_specs=out_specs,
            out_shape=out_shape,
            input_output_aliases=alias,
            cost_estimate=pl.CostEstimate(flops=WORK * elements, bytes_accessed=BYTES * elements, transcendentals=0),
            compiler_params=pltpu.CompilerParams(
                dimension_semantics=("arbitrary",), vmem_limit_bytes=32 * 1024 * 1024
            ),
        )(odd_arr, mobility, stiffness, *args, *tokens)

    far, sums_at = [], []

    def field_piece(index):
        array = initial if index < count else cotangent
        return cut(array, far_plane, (index % count) * size, size)

    def start_until(limit):
        while len(far) < min(limit, 2 * count):
            index = len(far)
            piece = field_piece(index) if index else first
            before = []
            if index >= IN_FLIGHT:
                before.append(far[index - IN_FLIGHT])
            if index > IN_FLIGHT and len(sums_at) > index - IN_FLIGHT - 1:
                before.append(sums_at[index - IN_FLIGHT - 1])
            sent = send_far(after(piece, *before))
            far.extend([sent] * (joined if index == 0 else 1))

    first = cut(initial, far_plane, 0, joined * size)
    squares_first = order_sum(jnp.sum(initial * initial, 0))
    near_share = NEAR_SHARE if count % NEAR_SHARE == 0 else 1
    near = []

    def near_until(index):
        while len(near) * near_share <= index:
            piece = len(near) * near_share
            array = initial if piece < count else cotangent
            plane = cut(array, near_plane, (piece % count) * size, near_share * size)
            before = [far[piece - NEAR_LAG]] if piece >= NEAR_LAG else ([first] if FIRST else [])
            near.append(send_near(after(plane, *before)))

    start_until(IN_FLIGHT)
    if EARLY:
        near_until(2 * count - 1)

    middle, sums = [], None
    for k in range(count):
        start_until(IN_FLIGHT + k)
        near_until(k)
        fresh = k == 0
        value, sums = call(
            middle_kernel, k, fresh,
            [slab_at(k * size), slab_at(k * size), plane_at(k * size if k < joined else 0),
             plane_at((k % near_share) * size), cell_spec]
            + ([] if fresh else [cells_spec]),
            [initial, cotangent, far[k], near[k // near_share], squares_first] + ([] if fresh else [sums]),
            [slab_at(0), cells_spec], [slab, cells], {} if fresh else {8: 1},
        )
        middle.append(value)
        sums_at.append(sums)
    start_until(2 * count)
    near_until(2 * count - 1)
    sums = order_sum(sums)

    outs, coupled, held = [], None, None
    back, back_near, owns = [], [], []
    groups = BACK_GROUPS if sum(BACK_GROUPS) == count else (1,) * count
    opens = [sum(groups[:g]) for g in range(len(groups))]
    group_of = [g for g, members in enumerate(groups) for _ in range(members)]
    for k in range(count):
        fresh, group = k == 0, group_of[k]
        inside = (k - opens[group]) * size
        specs = [slab_at(k * size), slab_at(0), slab_at(k * size), plane_at(0), plane_at((k % near_share) * size), cell_spec, cells_spec]
        args = [initial, middle[k], cotangent, far[count + k], near[(count + k) // near_share], squares_first, sums]
        tokens = []
        if BACK and k >= BACK and k - BACK < len(back):
            tokens = [back[k - BACK]]
        alias = {}
        if not fresh:
            specs, args = specs + [cell_spec], args + [coupled]
            alias[3 + len(args) - 1] = 3
        if k != opens[group]:
            specs, args = specs + [anywhere], args + [held]
            alias[3 + len(args) - 1] = 1
        outer, held, own, coupled = call(
            adjoint_kernel, k, fresh, specs, args,
            [plane_at(0), plane_at(inside), slab_at(0), cell_spec],
            [plane_out, shape(groups[group] * size, rows, columns), slab, cell], alias, tokens,
        )
        owns.append(own)
        outs.append(outer)
        if k <= AHEAD or not CARRY:
            back.append(send_far(outer))
        if k + 1 == opens[group] + groups[group]:
            plane = held
            back_near.append(send_near(plane))
    coupled = order_sum(coupled)

    result = None
    for k in range(count):
        fresh, group = k == 0, group_of[k]
        inside = (k - opens[group]) * size
        later = len(back) if CARRY and len(back) < count else None
        specs = [slab_at(k * size), plane_at(0), plane_at(inside), cell_spec, slab_at(0)]
        args = [initial, back[k], back_near[group], coupled, owns[k]]
        out_specs, out_shape, alias = [slab_at(k * size)], [shape(*initial.shape)], {}
        if not fresh:
            specs, args = specs + [anywhere], args + [result]
            alias[3 + len(args) - 1] = 0
        if later is not None:
            specs, args = specs + [anywhere], args + [outs[later]]
            out_specs, out_shape = out_specs + [anywhere], out_shape + [plane_out]
            alias[3 + len(args) - 1] = 1
        result, *handed = call(last_kernel, k, fresh, specs, args, out_specs, out_shape, alias)
        if later is not None:
            back.append(send_far(handed[0]))
    return result


def solution(mesh):
    return jax.shard_map(
        on_device,
        mesh=mesh,
        in_specs=(P("ord", "gz", None, None), P("ord", "gz", None, None), P("ord"), P("ord")),
        out_specs=P("ord", "gz", None, None),
        check_vma=False,
    )
```
